32 devices in a mesh: mesh: 16 (over z, x, core), modes: 2 (over y).
Axes of the slice: x: 2, y: 2, z: 4, core: 2. Of those that a mesh axis runs over, the one named last changes fastest.
Arguments:
- subspace: float32 [64, 3, 16, 9216], P('modes', None, 'mesh'), may hold values from -14 to 14
- classes: int32 [16, 9216], P('mesh'), may hold values from 0 to 15
- level_density: float32 [16], replicated, may hold values from 0.05 to 1
Outputs:
- residual: float32 [64, 3, 16, 9216], P('modes', None, 'mesh')
- ritz_matrix: float32 [64, 64], replicated
The draws below stay inside these ranges and needn't reach their ends.
All inputs are finite; a program needn't handle non-finite values.
Results may differ from the reference program's by a relative error of at most 0.0003.
Values sent between devices are 32-bit elements; how exact they have to be, the bound alone decides.
A program may use at most 128 MiB of HBM per device.

```python
import math
import jax
import jax.numpy as jnp
import numpy as np
from jax import lax

MODES = 64
NX = 96
NY = 96
LEVELS = 16
NZ = 16
NDOF = 442368


def draw_subspace(key, part):
    base = jax.random.fold_in(key, 17)
    key_noise, key_common, key_weight = jax.random.split(base, 3)
    array_shape = (MODES, 3, NZ, NX * NY)
    plane_index = jnp.arange(NZ, dtype=jnp.float32) / max(NZ - 1, 1)
    random_part = jax.random.truncated_normal(key_noise, -4.0, 4.0, array_shape, jnp.float32)
    common = jax.random.truncated_normal(key_common, -4.0, 4.0, (1, 3, NZ, NX * NY), jnp.float32)
    amplitude = 1.0 + 0.75 * plane_index
    mode_weight = jax.random.uniform(key_weight, (MODES, 1, 1, 1), jnp.float32, 0.3, 0.9)
    return ((random_part + mode_weight * common) * amplitude[None, None, :, None]).astype(jnp.float32)


def plant(array, rng, smallest, high):
    shape = array.shape
    spot = [jax.random.randint(jax.random.fold_in(rng, axis), (), 0, shape[axis]) for axis in range(len(shape))]
    array = array.at[tuple(spot)].set(smallest)
    longest = shape.index(max(shape))
    spot[longest] = (spot[longest] + 1) % shape[longest]
    return array.at[tuple(spot)].set(high)


def setup_inputs(seed: int = 0) -> dict:
    streams_of = jax.random.split(jax.random.key(seed), 4)
    return {
        "subspace": draw_subspace(jax.random.fold_in(streams_of[3], 71), 0),
        "classes": plant(jax.random.randint(streams_of[1], (NZ, NX * NY), 0, LEVELS), jax.random.fold_in(streams_of[1], 1), 0, LEVELS - 1).astype(jnp.int32),
        "level_density": jnp.clip(jnp.exp(jax.random.uniform(streams_of[2], (LEVELS,), jnp.float32, math.log(0.05), math.log(1.0))), 0.05, 1.0),
    }


highest = lax.Precision.HIGHEST
floor_modulus = 0.001
penalty_power = 3.0

def element_matrix():
    poisson_ratio = 0.3
    lame_first = poisson_ratio / ((1 + poisson_ratio) * (1 - 2 * poisson_ratio))
    shear_modulus = 1.0 / (2 * (1 + poisson_ratio))
    elastic = np.zeros((6, 6))
    elastic[:3, :3] = lame_first
    for normal_index in range(3):
        elastic[normal_index, normal_index] = lame_first + 2 * shear_modulus
        elastic[normal_index + 3, normal_index + 3] = shear_modulus
    corner_signs = [(1 - 2 * (corner & 1), 1 - 2 * (corner >> 1 & 1), 1 - 2 * (corner >> 2)) for corner in range(8)]
    gauss_point = 1.0 / np.sqrt(3.0)
    matrix = np.zeros((24, 24))
    for gauss_x in (-gauss_point, gauss_point):
        for gauss_y in (-gauss_point, gauss_point):
            for gauss_z in (-gauss_point, gauss_point):
                strain = np.zeros((6, 24))
                for corner in range(8):
                    sign_x, sign_y, sign_z = corner_signs[corner]
                    deriv_x = 2 * sign_x * (1 + sign_y * gauss_y) * (1 + sign_z * gauss_z) / 8
                    deriv_y = 2 * sign_y * (1 + sign_x * gauss_x) * (1 + sign_z * gauss_z) / 8
                    deriv_z = 2 * sign_z * (1 + sign_x * gauss_x) * (1 + sign_y * gauss_y) / 8
                    column = 3 * corner
                    strain[0, column] = deriv_x
                    strain[1, column + 1] = deriv_y
                    strain[2, column + 2] = deriv_z
                    strain[3, column] = deriv_y
                    strain[3, column + 1] = deriv_x
                    strain[4, column + 1] = deriv_z
                    strain[4, column + 2] = deriv_y
                    strain[5, column] = deriv_z
                    strain[5, column + 2] = deriv_x
                matrix = matrix + strain.T @ elastic @ strain / 8
    return matrix.reshape(8, 3, 8, 3)

def shift_in(plane, step_x, step_y, width_x):
    offset = step_x + step_y * width_x
    moved = plane
    if offset > 0:
        moved = jnp.pad(plane[..., :-offset], [(0, 0)] * (plane.ndim - 1) + [(offset, 0)])
    if step_x:
        column = lax.iota(jnp.int32, plane.shape[-1]) % width_x
        moved = jnp.where(column >= 1, moved, 0.0)
    return moved

def shift_out(force, step_x, step_y, width_x):
    moved = force
    if step_x:
        column = lax.iota(jnp.int32, force.shape[-1]) % width_x
        moved = jnp.where(column >= 1, moved, 0.0)
    offset = step_x + step_y * width_x
    if offset > 0:
        moved = jnp.pad(moved[..., offset:], [(0, 0)] * (force.ndim - 1) + [(0, offset)])
    return moved

def layer_forces(bottom, top, modulus_row, element, width_x):
    corners = []
    for step_z in (0, 1):
        source = top if step_z == 0 else bottom
        for step_y in (0, 1):
            for step_x in (0, 1):
                corners.append(shift_in(source, step_x, step_y, width_x))
    stacked = jnp.stack(corners, 0)
    forces = jnp.einsum('acbd,bkdn->akcn', element, stacked, precision=highest) * modulus_row
    force_top = jnp.zeros_like(top)
    force_bottom = jnp.zeros_like(bottom)
    for corner in range(8):
        moved_force = shift_out(forces[corner], corner & 1, corner >> 1 & 1, width_x)
        if corner >> 2 == 0:
            force_top = force_top + moved_force
        else:
            force_bottom = force_bottom + moved_force
    return (force_bottom, force_top)

def densities(classes, level_density):
    levels = level_density.shape[0]
    level_index = lax.iota(jnp.int32, levels).reshape(levels, 1, 1)
    matches = classes[None] == level_index
    return lax.optimization_barrier(jnp.sum(jnp.where(matches, level_density[:, None, None], 0.0), 0))

def ritz_solve(gram_stiff, gram_mass):
    lower_factor = jnp.linalg.cholesky(gram_mass)
    identity = jnp.eye(gram_mass.shape[0], dtype=jnp.float32)
    inverse = jax.scipy.linalg.solve_triangular(lower_factor, identity, lower=True)
    rotate = inverse.T
    ritz_matrix = jnp.dot(jnp.dot(inverse.astype(jnp.float32), gram_stiff.astype(jnp.float32), precision=highest, preferred_element_type=jnp.float32).astype(jnp.float32), rotate.astype(jnp.float32), precision=highest, preferred_element_type=jnp.float32)
    mixed_rotate = jnp.dot(rotate.astype(jnp.float32), ritz_matrix.astype(jnp.float32), precision=highest, preferred_element_type=jnp.float32)
    return (ritz_matrix, rotate, mixed_rotate)

def reference(subspace, classes, level_density):
    element = jnp.asarray(element_matrix(), jnp.float32)
    density = densities(classes, level_density)
    modulus = floor_modulus + (1.0 - floor_modulus) * density * density * density
    planes = jnp.moveaxis(subspace, 2, 0)
    below_planes = jnp.concatenate([jnp.zeros_like(planes[:1]), planes[:-1]], 0)

    def layer_step(carry, inputs):
        bottom, top, modulus_row = inputs
        return (carry, layer_forces(bottom, top, modulus_row, element, NX))
    unused, (force_bottom, force_top) = lax.scan(layer_step, jnp.zeros((), jnp.float32), (below_planes, planes, modulus))
    image_planes = force_top + jnp.concatenate([force_bottom[1:], jnp.zeros_like(force_bottom[:1])], 0)
    stiff_image = jnp.moveaxis(image_planes, 0, 2)
    mass_basis = subspace * density[None, None]
    gram_stiff = jnp.einsum('kczn,jczn->kj', subspace, stiff_image, precision=highest) / NDOF
    gram_mass = jnp.einsum('kczn,jczn->kj', subspace, mass_basis, precision=highest) / NDOF
    ritz_matrix, rotate, mixed_rotate = ritz_solve(gram_stiff, gram_mass)
    residual = jnp.einsum('kczn,kj->jczn', stiff_image, rotate, precision=highest) - jnp.einsum('kczn,kj->jczn', mass_basis, mixed_rotate, precision=highest)
    return (residual, ritz_matrix)
```

```python
import functools

import jax
import jax.numpy as jnp
import numpy as np
from jax import lax
from jax.experimental import pallas as pl
from jax.experimental.pallas import tpu as pltpu
from jax.sharding import PartitionSpec as P

NX = 96
NY = 96


highest = lax.Precision.HIGHEST
high = lax.Precision.HIGH
MARGIN = 128
floor_modulus = 0.001


def shifted(x, axis, by):
    size = lax.axis_size(axis)
    pairs = [(i, i + by) for i in range(size) if 0 <= i + by < size]
    return lax.ppermute(x, axis, pairs)


def element_matrix():
    poisson_ratio = 0.3
    lame_first = poisson_ratio / ((1 + poisson_ratio) * (1 - 2 * poisson_ratio))
    shear_modulus = 1.0 / (2 * (1 + poisson_ratio))
    elastic = np.zeros((6, 6))
    elastic[:3, :3] = lame_first
    for normal_index in range(3):
        elastic[normal_index, normal_index] = lame_first + 2 * shear_modulus
        elastic[normal_index + 3, normal_index + 3] = shear_modulus
    corner_signs = [
        (1 - 2 * (corner & 1), 1 - 2 * (corner >> 1 & 1), 1 - 2 * (corner >> 2))
        for corner in range(8)
    ]
    gauss_point = 1.0 / np.sqrt(3.0)
    matrix = np.zeros((24, 24))
    for gauss_x in (-gauss_point, gauss_point):
        for gauss_y in (-gauss_point, gauss_point):
            for gauss_z in (-gauss_point, gauss_point):
                strain = np.zeros((6, 24))
                for corner in range(8):
                    sign_x, sign_y, sign_z = corner_signs[corner]
                    deriv_x = 2 * sign_x * (1 + sign_y * gauss_y) * (1 + sign_z * gauss_z) / 8
                    deriv_y = 2 * sign_y * (1 + sign_x * gauss_x) * (1 + sign_z * gauss_z) / 8
                    deriv_z = 2 * sign_z * (1 + sign_x * gauss_x) * (1 + sign_y * gauss_y) / 8
                    column = 3 * corner
                    strain[0, column] = deriv_x
                    strain[1, column + 1] = deriv_y
                    strain[2, column + 2] = deriv_z
                    strain[3, column] = deriv_y
                    strain[3, column + 1] = deriv_x
                    strain[4, column + 1] = deriv_z
                    strain[4, column + 2] = deriv_y
                    strain[5, column] = deriv_z
                    strain[5, column + 2] = deriv_x
                matrix = matrix + strain.T @ elastic @ strain / 8
    return matrix.reshape(8, 3, 8, 3)


def hadamard_matrix():
    signs = np.array([[1.0, 1.0], [1.0, -1.0]])
    transform = np.kron(np.kron(signs, signs), signs)
    matrix = np.einsum("ha,acbd,bg->hcgd", transform, element_matrix(), transform) / 64
    matrix[np.abs(matrix) < 1e-12] = 0.0
    return matrix


def layer_kernel(chunk, lanes_own, top_ref, bottom_ref, modulus_ref, inside_ref, out_top, out_bottom):
    matrix = hadamard_matrix()

    def step(index, carry):
        start = pl.multiple_of(index * chunk, 128)
        wide = chunk + 2 * MARGIN
        narrow = chunk + MARGIN
        inside = inside_ref[:, pl.ds(start, wide)]
        modulus = modulus_ref[:, pl.ds(start + MARGIN, narrow)]
        inside_narrow = inside[:, MARGIN:]
        hat = {}
        for c in range(3):
            top = top_ref[c, :, pl.ds(start, wide)]
            bottom = bottom_ref[c, :, pl.ds(start, wide)]
            for hz, plane in ((0, top + bottom), (1, top - bottom)):
                moved = pltpu.roll(plane, 1, 1) * inside
                for hx, line in ((0, plane + moved), (1, plane - moved)):
                    here = line[:, MARGIN:]
                    behind = pltpu.roll(line, NX, 1)[:, MARGIN:]
                    hat[hx + 4 * hz, c] = here + behind
                    hat[hx + 2 + 4 * hz, c] = here - behind

        def force(h, c):
            total = None
            for g in range(8):
                for d in range(3):
                    factor = float(matrix[h, c, g, d])
                    if factor != 0.0:
                        term = hat[g, d] * factor
                        total = term if total is None else total + term
            return None if total is None else total * modulus

        def both(first, second):
            if first is None:
                return second, -second
            return first + second, first - second

        for c in range(3):
            layers = []
            for hz in (0, 1):
                lines = []
                for hx in (0, 1):
                    near, far = both(force(hx + 4 * hz, c), force(hx + 2 + 4 * hz, c))
                    lines.append(near + pltpu.roll(far, narrow - NX, 1))
                near, far = both(lines[0], lines[1])
                layers.append((near + pltpu.roll(far * inside_narrow, narrow - 1, 1))[:, :chunk])
            out_top[c, :, pl.ds(start, chunk)] = layers[0] + layers[1]
            out_bottom[c, :, pl.ds(start, chunk)] = layers[0] - layers[1]
        return carry

    lax.fori_loop(0, lanes_own // chunk, step, 0)


def layer_forces(top, bottom, modulus, inside):
    comps, mode_count, wide = top.shape
    lanes_own = wide - 2 * MARGIN
    chunk = CHUNK if lanes_own % CHUNK == 0 else 128
    rows = 8
    in_block = pl.BlockSpec((comps, rows, wide), lambda m: (0, m, 0))
    row_block = pl.BlockSpec((1, wide), lambda m: (0, 0))
    out_block = pl.BlockSpec((comps, rows, lanes_own), lambda m: (0, m, 0))
    shape = jax.ShapeDtypeStruct((comps, mode_count, lanes_own), jnp.float32)
    return pl.pallas_call(
        functools.partial(layer_kernel, chunk, lanes_own),
        grid=(mode_count // rows,),
        in_specs=[in_block, in_block, row_block, row_block],
        out_specs=[out_block, out_block],
        out_shape=[shape, shape],
        cost_estimate=pl.CostEstimate(
            flops=240 * top.size, bytes_accessed=16 * top.size, transcendentals=0
        ),
        compiler_params=pltpu.CompilerParams(vmem_limit_bytes=32 * 2**20),
    )(top, bottom, modulus, inside)


CHUNK = 1152


def densities(classes, level_density):
    levels = level_density.shape[0]
    level_index = lax.iota(jnp.int32, levels).reshape(levels, 1, 1)
    matches = classes[None] == level_index
    return jnp.sum(jnp.where(matches, level_density[:, None, None], 0.0), 0)


def ritz_solve(gram_stiff, gram_mass):
    lower_factor = jnp.linalg.cholesky(gram_mass)
    identity = jnp.eye(gram_mass.shape[0], dtype=jnp.float32)
    inverse = jax.scipy.linalg.solve_triangular(lower_factor, identity, lower=True)
    rotate = inverse.T
    ritz_matrix = jnp.dot(
        jnp.dot(inverse, gram_stiff, precision=highest, preferred_element_type=jnp.float32),
        rotate,
        precision=highest,
        preferred_element_type=jnp.float32,
    )
    mixed_rotate = jnp.dot(
        rotate, ritz_matrix, precision=highest, preferred_element_type=jnp.float32
    )
    return (ritz_matrix, rotate, mixed_rotate)


def rotated(x, axis, by):
    size = lax.axis_size(axis)
    return lax.ppermute(x, axis, [(i, (i + by) % size) for i in range(size)])


def per_device(subspace, classes, level_density):
    mode_count, comps, plane_count, nodes = subspace.shape
    groups = lax.axis_size("modes")
    group = lax.axis_index("modes")
    total_dofs = comps * nodes * plane_count * lax.axis_size("mesh")
    lanes_own = nodes // groups
    wide = lanes_own + 2 * MARGIN

    density = densities(classes, level_density)
    modulus = floor_modulus + (1.0 - floor_modulus) * density * density * density
    own = group * lanes_own
    modulus = lax.dynamic_slice(jnp.pad(modulus, ((0, 0), (MARGIN, MARGIN))), (0, own), (1, wide))
    density = lax.dynamic_slice(density, (0, own), (1, lanes_own))
    inside = jnp.asarray(((np.arange(wide) - MARGIN) % NX >= 1)[None], jnp.float32)

    vectors = jnp.transpose(subspace[:, :, 0], (1, 0, 2))
    padded = jnp.pad(vectors, ((0, 0), (0, 0), (MARGIN, MARGIN)))
    tops, forces, bottoms = [], [], []
    for s in range(groups):
        target = lax.rem(group + s, groups)
        window = lax.dynamic_slice(
            padded, (0, 0, target * lanes_own), (comps, mode_count, wide)
        )
        top = window if s == 0 else rotated(window, "modes", s)
        tops.append(top)
        bottoms.append(shifted(top, "mesh", 1))
    for top, bottom in zip(tops, bottoms):
        forces.append(layer_forces(top, bottom, modulus, inside))
    returned = [shifted(force[1], "mesh", -1) for force in forces]
    middle = slice(MARGIN, MARGIN + lanes_own)
    top = jnp.concatenate([t[:, :, middle] for t in tops], 1)
    bottom = jnp.concatenate([b[:, :, middle] for b in bottoms], 1)
    force_top = jnp.concatenate([f[0] for f in forces], 1)
    force_bottom = jnp.concatenate([f[1] for f in forces], 1)
    mass = top * density

    def gram(a, b):
        return jnp.einsum("ckn,cjn->kj", a, b, precision=high)

    part_stiff = gram(top, force_top) + gram(bottom, force_bottom)
    part_mass = gram(top, mass)
    order = lax.rem(
        lax.rem(group - lax.iota(jnp.int32, groups) + groups, groups)[:, None] * mode_count
        + lax.iota(jnp.int32, mode_count)[None],
        groups * mode_count,
    ).reshape(-1)
    place = (order[:, None] == lax.iota(jnp.int32, groups * mode_count)[None]).astype(jnp.float32)

    def absolute(matrix):
        return jnp.dot(jnp.dot(place.T, matrix, precision=highest), place, precision=highest)

    def relative(matrix):
        return jnp.dot(jnp.dot(place, matrix, precision=highest), place.T, precision=highest)

    gram_stiff, gram_mass = lax.psum(
        (absolute(part_stiff), absolute(part_mass)), ("mesh", "modes")
    )
    ritz_matrix, rotate, mixed_rotate = ritz_solve(gram_stiff / total_dofs, gram_mass / total_dofs)
    rotate = relative(rotate)
    mixed_rotate = relative(mixed_rotate)
    image = force_top + jnp.concatenate(returned, 1)
    parts = []
    for s in reversed(range(groups)):
        columns = slice(s * mode_count, (s + 1) * mode_count)
        part = jnp.einsum("ckn,kj->jcn", image, rotate[:, columns], precision=high)
        part = part - jnp.einsum("ckn,kj->jcn", mass, mixed_rotate[:, columns], precision=high)
        parts.append(part if s == 0 else rotated(part, "modes", -s))
    parts = parts[::-1]
    residual = jnp.zeros((mode_count, comps, nodes), jnp.float32)
    for s, part in enumerate(parts):
        source = lax.rem(group + s, groups)
        residual = lax.dynamic_update_slice(residual, part, (0, 0, source * lanes_own))
    return (residual[:, :, None], ritz_matrix)


def solution(mesh):
    in_specs = (P("modes", None, "mesh", None), P("mesh", None), P())
    out_specs = (P("modes", None, "mesh", None), P())
    return jax.shard_map(
        per_device, mesh=mesh, in_specs=in_specs, out_specs=out_specs, check_vma=False
    )
```

```python
import functools

import jax
import jax.numpy as jnp
import numpy as np
from jax import lax
from jax.experimental import pallas as pl
from jax.experimental.pallas import tpu as pltpu
from jax.sharding import PartitionSpec as P

NX = 96
NY = 96


highest = lax.Precision.HIGHEST
high = lax.Precision.HIGH
MARGIN = 128
floor_modulus = 0.001


def shifted(x, axis, by):
    size = lax.axis_size(axis)
    pairs = [(i, i + by) for i in range(size) if 0 <= i + by < size]
    return lax.ppermute(x, axis, pairs)


def element_matrix():
    poisson_ratio = 0.3
    lame_first = poisson_ratio / ((1 + poisson_ratio) * (1 - 2 * poisson_ratio))
    shear_modulus = 1.0 / (2 * (1 + poisson_ratio))
    elastic = np.zeros((6, 6))
    elastic[:3, :3] = lame_first
    for normal_index in range(3):
        elastic[normal_index, normal_index] = lame_first + 2 * shear_modulus
        elastic[normal_index + 3, normal_index + 3] = shear_modulus
    corner_signs = [
        (1 - 2 * (corner & 1), 1 - 2 * (corner >> 1 & 1), 1 - 2 * (corner >> 2))
        for corner in range(8)
    ]
    gauss_point = 1.0 / np.sqrt(3.0)
    matrix = np.zeros((24, 24))
    for gauss_x in (-gauss_point, gauss_point):
        for gauss_y in (-gauss_point, gauss_point):
            for gauss_z in (-gauss_point, gauss_point):
                strain = np.zeros((6, 24))
                for corner in range(8):
                    sign_x, sign_y, sign_z = corner_signs[corner]
                    deriv_x = 2 * sign_x * (1 + sign_y * gauss_y) * (1 + sign_z * gauss_z) / 8
                    deriv_y = 2 * sign_y * (1 + sign_x * gauss_x) * (1 + sign_z * gauss_z) / 8
                    deriv_z = 2 * sign_z * (1 + sign_x * gauss_x) * (1 + sign_y * gauss_y) / 8
                    column = 3 * corner
                    strain[0, column] = deriv_x
                    strain[1, column + 1] = deriv_y
                    strain[2, column + 2] = deriv_z
                    strain[3, column] = deriv_y
                    strain[3, column + 1] = deriv_x
                    strain[4, column + 1] = deriv_z
                    strain[4, column + 2] = deriv_y
                    strain[5, column] = deriv_z
                    strain[5, column + 2] = deriv_x
                matrix = matrix + strain.T @ elastic @ strain / 8
    return matrix.reshape(8, 3, 8, 3)


def hadamard_matrix():
    signs = np.array([[1.0, 1.0], [1.0, -1.0]])
    transform = np.kron(np.kron(signs, signs), signs)
    matrix = np.einsum("ha,acbd,bg->hcgd", transform, element_matrix(), transform) / 64
    matrix[np.abs(matrix) < 1e-12] = 0.0
    return matrix


def layer_kernel(chunk, lanes_own, top_ref, bottom_ref, modulus_ref, inside_ref, out_top, out_bottom):
    matrix = hadamard_matrix()

    def step(index, carry):
        start = pl.multiple_of(index * chunk, 128)
        wide = chunk + 2 * MARGIN
        narrow = chunk + MARGIN
        inside = inside_ref[:, pl.ds(start, wide)]
        modulus = modulus_ref[:, pl.ds(start + MARGIN, narrow)]
        inside_narrow = inside[:, MARGIN:]
        hat = {}
        for c in range(3):
            top = top_ref[c, :, pl.ds(start, wide)]
            bottom = bottom_ref[c, :, pl.ds(start, wide)]
            for hz, plane in ((0, top + bottom), (1, top - bottom)):
                moved = pltpu.roll(plane, 1, 1) * inside
                for hx, line in ((0, plane + moved), (1, plane - moved)):
                    here = line[:, MARGIN:]
                    behind = pltpu.roll(line, NX, 1)[:, MARGIN:]
                    hat[hx + 4 * hz, c] = here + behind
                    hat[hx + 2 + 4 * hz, c] = here - behind

        def force(h, c):
            total = None
            for g in range(8):
                for d in range(3):
                    factor = float(matrix[h, c, g, d])
                    if factor != 0.0:
                        term = hat[g, d] * factor
                        total = term if total is None else total + term
            return None if total is None else total * modulus

        def both(first, second):
            if first is None:
                return second, -second
            return first + second, first - second

        for c in range(3):
            layers = []
            for hz in (0, 1):
                lines = []
                for hx in (0, 1):
                    near, far = both(force(hx + 4 * hz, c), force(hx + 2 + 4 * hz, c))
                    lines.append(near + pltpu.roll(far, narrow - NX, 1))
                near, far = both(lines[0], lines[1])
                layers.append((near + pltpu.roll(far * inside_narrow, narrow - 1, 1))[:, :chunk])
            out_top[c, :, pl.ds(start, chunk)] = layers[0] + layers[1]
            out_bottom[c, :, pl.ds(start, chunk)] = layers[0] - layers[1]
        return carry

    lax.fori_loop(0, lanes_own // chunk, step, 0)


def layer_forces(top, bottom, modulus, inside):
    comps, mode_count, wide = top.shape
    lanes_own = wide - 2 * MARGIN
    chunk = next(size for size in CHUNKS if lanes_own % size == 0)
    rows = 8
    in_block = pl.BlockSpec((comps, rows, wide), lambda m: (0, m, 0))
    row_block = pl.BlockSpec((1, wide), lambda m: (0, 0))
    out_block = pl.BlockSpec((comps, rows, lanes_own), lambda m: (0, m, 0))
    shape = jax.ShapeDtypeStruct((comps, mode_count, lanes_own), jnp.float32)
    return pl.pallas_call(
        functools.partial(layer_kernel, chunk, lanes_own),
        grid=(mode_count // rows,),
        in_specs=[in_block, in_block, row_block, row_block],
        out_specs=[out_block, out_block],
        out_shape=[shape, shape],
        cost_estimate=pl.CostEstimate(
            flops=240 * top.size, bytes_accessed=16 * top.size, transcendentals=0
        ),
        compiler_params=pltpu.CompilerParams(vmem_limit_bytes=32 * 2**20),
    )(top, bottom, modulus, inside)


CHUNKS = (2304, 1152, 384, 128)


def densities(classes, level_density):
    levels = level_density.shape[0]
    level_index = lax.iota(jnp.int32, levels).reshape(levels, 1, 1)
    matches = classes[None] == level_index
    return jnp.sum(jnp.where(matches, level_density[:, None, None], 0.0), 0)


def dot(a, b, contract):
    return lax.dot_general(
        a, b, ((contract[:1], contract[1:]), ((), ())), precision=highest,
        preferred_element_type=jnp.float32,
    )


def ritz_kernel(
    axes, mode_count, total_dofs, stiff_ref, mass_ref, ritz_ref, rotate_ref, mixed_ref,
    sums, landed, send_sem, recv_sem,
):
    size = stiff_ref.shape[0]
    groups = size // mode_count
    partners = []
    for name, count in axes:
        own = lax.axis_index(name)
        bit = 1
        while bit < count:
            set_here = lax.rem(lax.div(own, bit), 2)
            partners.append({name: own + bit - 2 * bit * set_here})
            bit *= 2
    barrier = pltpu.get_barrier_semaphore()
    for partner in partners:
        pl.semaphore_signal(
            barrier, inc=1, device_id=partner, device_id_type=pl.DeviceIdType.MESH
        )

    group = lax.axis_index("modes")
    row = lax.broadcasted_iota(jnp.int32, (size, size), 0)
    column = lax.broadcasted_iota(jnp.int32, (size, size), 1)
    place = jnp.zeros((size, size), jnp.float32)
    for s in range(groups):
        move = (lax.rem(group - s + groups, groups) - s) * mode_count
        here = (row >= s * mode_count) & (row < (s + 1) * mode_count) & (column - row == move)
        place = jnp.where(here, 1.0, place)

    sums[0, :, :size] = dot(dot(place, stiff_ref[...], (0, 0)), place, (1, 0))
    sums[0, :, size:] = dot(dot(place, mass_ref[...], (0, 0)), place, (1, 0))
    pl.semaphore_wait(barrier, len(partners))
    for step, partner in enumerate(partners):
        copy = pltpu.make_async_remote_copy(
            src_ref=sums.at[step],
            dst_ref=landed.at[step],
            send_sem=send_sem.at[step],
            recv_sem=recv_sem.at[step],
            device_id=partner,
            device_id_type=pl.DeviceIdType.MESH,
        )
        copy.start()
        copy.wait()
        sums[step + 1] = sums[step] + landed[step]
    total = sums[len(partners)] * (1.0 / total_dofs)
    gram_stiff = total[:, :size]

    lane = lax.broadcasted_iota(jnp.int32, (8, 2 * size), 1)
    sub = lax.broadcasted_iota(jnp.int32, (8, 2 * size), 0)
    blocks = []
    for block in range(size // 8):
        unit = jnp.where(lane == sub + 8 * block, 1.0, 0.0)
        blocks.append(jnp.where(lane < size, unit, total[8 * block : 8 * block + 8]))
    for k in range(size):
        at = k // 8
        pivot_row = blocks[at][k % 8 : k % 8 + 1]
        pivot_row = pivot_row / pivot_row[:, size + k : size + k + 1]
        for block in range(at, size // 8):
            factor = blocks[block][:, size + k : size + k + 1]
            if block == at:
                factor = jnp.where(sub[:, :1] > k % 8, factor, 0.0)
            blocks[block] = blocks[block] - factor * pivot_row
    rows = jnp.concatenate(blocks, 0)
    row = lax.broadcasted_iota(jnp.int32, (size, 2 * size), 0)
    column = lax.broadcasted_iota(jnp.int32, (size, 2 * size), 1)
    pivots = jnp.sum(jnp.where(column == row + size, rows, 0.0), 1, keepdims=True)
    inverse = rows[:, :size] * (1.0 / jnp.sqrt(pivots))
    ritz = dot(dot(inverse, gram_stiff, (1, 0)), inverse, (1, 1))
    ritz_ref[...] = ritz
    mixed = dot(ritz, inverse, (0, 0))
    rotate_ref[...] = dot(dot(place, inverse, (1, 0)), place, (1, 1))
    mixed_ref[...] = dot(dot(place, mixed, (1, 0)), place, (1, 1))


def ritz_solve(part_stiff, part_mass, mode_count, total_dofs):
    size = part_stiff.shape[0]
    axes = [(name, lax.axis_size(name)) for name in ("mesh", "modes")]
    steps = sum(count.bit_length() - 1 for name, count in axes)
    shape = jax.ShapeDtypeStruct((size, size), jnp.float32)
    whole = pl.BlockSpec(memory_space=pltpu.VMEM)
    return pl.pallas_call(
        functools.partial(ritz_kernel, axes, mode_count, total_dofs),
        in_specs=[whole, whole],
        out_specs=[whole] * 3,
        out_shape=[shape] * 3,
        scratch_shapes=[
            pltpu.VMEM((steps + 1, size, 2 * size), jnp.float32),
            pltpu.VMEM((steps, size, 2 * size), jnp.float32),
            pltpu.SemaphoreType.DMA((steps,)),
            pltpu.SemaphoreType.DMA((steps,)),
        ],
        cost_estimate=pl.CostEstimate(flops=10**7, bytes_accessed=10**5, transcendentals=0),
        compiler_params=pltpu.CompilerParams(collective_id=0, has_side_effects=True),
    )(part_stiff, part_mass)


def rotated(x, axis, by):
    size = lax.axis_size(axis)
    return lax.ppermute(x, axis, [(i, (i + by) % size) for i in range(size)])


def per_device(subspace, classes, level_density):
    mode_count, comps, plane_count, nodes = subspace.shape
    groups = lax.axis_size("modes")
    group = lax.axis_index("modes")
    total_dofs = comps * nodes * plane_count * lax.axis_size("mesh")
    lanes_own = nodes // groups
    wide = lanes_own + 2 * MARGIN

    density = densities(classes, level_density)
    modulus = floor_modulus + (1.0 - floor_modulus) * density * density * density
    own = group * lanes_own
    modulus = lax.dynamic_slice(jnp.pad(modulus, ((0, 0), (MARGIN, MARGIN))), (0, own), (1, wide))
    density = lax.dynamic_slice(density, (0, own), (1, lanes_own))
    inside = jnp.asarray(((np.arange(wide) - MARGIN) % NX >= 1)[None], jnp.float32)

    vectors = jnp.transpose(subspace[:, :, 0], (1, 0, 2))
    padded = jnp.pad(vectors, ((0, 0), (0, 0), (MARGIN, MARGIN)))
    tops, forces, bottoms = [], [], []
    for s in range(groups):
        target = lax.rem(group + s, groups)
        window = lax.dynamic_slice(
            padded, (0, 0, target * lanes_own), (comps, mode_count, wide)
        )
        top = window if s == 0 else rotated(window, "modes", s)
        tops.append(top)
        bottoms.append(shifted(top, "mesh", 1))
    for top, bottom in zip(tops, bottoms):
        forces.append(layer_forces(top, bottom, modulus, inside))
    returned = [shifted(force[1], "mesh", -1) for force in forces]
    middle = slice(MARGIN, MARGIN + lanes_own)
    top = jnp.concatenate([t[:, :, middle] for t in tops], 1)
    bottom = jnp.concatenate([b[:, :, middle] for b in bottoms], 1)
    force_top = jnp.concatenate([f[0] for f in forces], 1)
    force_bottom = jnp.concatenate([f[1] for f in forces], 1)
    mass = top * density

    def gram(a, b):
        return jnp.einsum("ckn,cjn->kj", a, b, precision=high)

    part_stiff = gram(top, force_top) + gram(bottom, force_bottom)
    part_mass = gram(top, mass)
    ritz_matrix, rotate, mixed_rotate = ritz_solve(part_stiff, part_mass, mode_count, total_dofs)
    image = force_top + jnp.concatenate(returned, 1)
    parts = []
    for s in reversed(range(groups)):
        columns = slice(s * mode_count, (s + 1) * mode_count)
        part = jnp.einsum("ckn,jk->jcn", image, rotate[columns], precision=high)
        part = part - jnp.einsum("ckn,jk->jcn", mass, mixed_rotate[columns], precision=high)
        parts.append(part if s == 0 else rotated(part, "modes", -s))
    parts = parts[::-1]
    residual = jnp.zeros((mode_count, comps, nodes), jnp.float32)
    for s, part in enumerate(parts):
        source = lax.rem(group + s, groups)
        residual = lax.dynamic_update_slice(residual, part, (0, 0, source * lanes_own))
    return (residual[:, :, None], ritz_matrix)


def solution(mesh):
    in_specs = (P("modes", None, "mesh", None), P("mesh", None), P())
    out_specs = (P("modes", None, "mesh", None), P())
    return jax.shard_map(
        per_device, mesh=mesh, in_specs=in_specs, out_specs=out_specs, check_vma=False
    )
```

```python
import functools

import jax
import jax.numpy as jnp
import numpy as np
from jax import lax
from jax.experimental import pallas as pl
from jax.experimental.pallas import tpu as pltpu
from jax.sharding import PartitionSpec as P

NX = 96
NY = 96


highest = lax.Precision.HIGHEST
high = lax.Precision.HIGH
MARGIN = 128
floor_modulus = 0.001


def shifted(x, axis, by):
    size = lax.axis_size(axis)
    pairs = [(i, i + by) for i in range(size) if 0 <= i + by < size]
    return lax.ppermute(x, axis, pairs)


def element_matrix():
    poisson_ratio = 0.3
    lame_first = poisson_ratio / ((1 + poisson_ratio) * (1 - 2 * poisson_ratio))
    shear_modulus = 1.0 / (2 * (1 + poisson_ratio))
    elastic = np.zeros((6, 6))
    elastic[:3, :3] = lame_first
    for normal_index in range(3):
        elastic[normal_index, normal_index] = lame_first + 2 * shear_modulus
        elastic[normal_index + 3, normal_index + 3] = shear_modulus
    corner_signs = [
        (1 - 2 * (corner & 1), 1 - 2 * (corner >> 1 & 1), 1 - 2 * (corner >> 2))
        for corner in range(8)
    ]
    gauss_point = 1.0 / np.sqrt(3.0)
    matrix = np.zeros((24, 24))
    for gauss_x in (-gauss_point, gauss_point):
        for gauss_y in (-gauss_point, gauss_point):
            for gauss_z in (-gauss_point, gauss_point):
                strain = np.zeros((6, 24))
                for corner in range(8):
                    sign_x, sign_y, sign_z = corner_signs[corner]
                    deriv_x = 2 * sign_x * (1 + sign_y * gauss_y) * (1 + sign_z * gauss_z) / 8
                    deriv_y = 2 * sign_y * (1 + sign_x * gauss_x) * (1 + sign_z * gauss_z) / 8
                    deriv_z = 2 * sign_z * (1 + sign_x * gauss_x) * (1 + sign_y * gauss_y) / 8
                    column = 3 * corner
                    strain[0, column] = deriv_x
                    strain[1, column + 1] = deriv_y
                    strain[2, column + 2] = deriv_z
                    strain[3, column] = deriv_y
                    strain[3, column + 1] = deriv_x
                    strain[4, column + 1] = deriv_z
                    strain[4, column + 2] = deriv_y
                    strain[5, column] = deriv_z
                    strain[5, column + 2] = deriv_x
                matrix = matrix + strain.T @ elastic @ strain / 8
    return matrix.reshape(8, 3, 8, 3)


def hadamard_matrix():
    signs = np.array([[1.0, 1.0], [1.0, -1.0]])
    transform = np.kron(np.kron(signs, signs), signs)
    matrix = np.einsum("ha,acbd,bg->hcgd", transform, element_matrix(), transform) / 64
    matrix[np.abs(matrix) < 1e-12] = 0.0
    return matrix


def layer_kernel(chunk, lanes_own, top_ref, bottom_ref, modulus_ref, inside_ref, out_top, out_bottom):
    matrix = hadamard_matrix()

    def step(index, carry):
        start = pl.multiple_of(index * chunk, 128)
        wide = chunk + 2 * MARGIN
        narrow = chunk + MARGIN
        inside = inside_ref[:, pl.ds(start, wide)]
        modulus = modulus_ref[:, pl.ds(start + MARGIN, narrow)]
        inside_narrow = inside[:, MARGIN:]
        hat = {}
        for c in range(3):
            top = top_ref[c, :, pl.ds(start, wide)]
            bottom = bottom_ref[c, :, pl.ds(start, wide)]
            for hz, plane in ((0, top + bottom), (1, top - bottom)):
                moved = pltpu.roll(plane, 1, 1) * inside
                for hx, line in ((0, plane + moved), (1, plane - moved)):
                    here = line[:, MARGIN:]
                    behind = pltpu.roll(line, NX, 1)[:, MARGIN:]
                    hat[hx + 4 * hz, c] = here + behind
                    hat[hx + 2 + 4 * hz, c] = here - behind

        def force(h, c):
            total = None
            for g in range(8):
                for d in range(3):
                    factor = float(matrix[h, c, g, d])
                    if factor != 0.0:
                        term = hat[g, d] * factor
                        total = term if total is None else total + term
            return None if total is None else total * modulus

        def both(first, second):
            if first is None:
                return second, -second
            return first + second, first - second

        for c in range(3):
            layers = []
            for hz in (0, 1):
                lines = []
                for hx in (0, 1):
                    near, far = both(force(hx + 4 * hz, c), force(hx + 2 + 4 * hz, c))
                    lines.append(near + pltpu.roll(far, narrow - NX, 1))
                near, far = both(lines[0], lines[1])
                layers.append((near + pltpu.roll(far * inside_narrow, narrow - 1, 1))[:, :chunk])
            out_top[c, :, pl.ds(start, chunk)] = layers[0] + layers[1]
            out_bottom[c, :, pl.ds(start, chunk)] = layers[0] - layers[1]
        return carry

    lax.fori_loop(0, lanes_own // chunk, step, 0)


def layer_forces(top, bottom, modulus, inside):
    comps, mode_count, wide = top.shape
    lanes_own = wide - 2 * MARGIN
    chunk = next(size for size in CHUNKS if lanes_own % size == 0)
    rows = 8
    in_block = pl.BlockSpec((comps, rows, wide), lambda m: (0, m, 0))
    row_block = pl.BlockSpec((1, wide), lambda m: (0, 0))
    out_block = pl.BlockSpec((comps, rows, lanes_own), lambda m: (0, m, 0))
    shape = jax.ShapeDtypeStruct((comps, mode_count, lanes_own), jnp.float32)
    return pl.pallas_call(
        functools.partial(layer_kernel, chunk, lanes_own),
        grid=(mode_count // rows,),
        in_specs=[in_block, in_block, row_block, row_block],
        out_specs=[out_block, out_block],
        out_shape=[shape, shape],
        cost_estimate=pl.CostEstimate(
            flops=36000 * top.size, bytes_accessed=16 * top.size, transcendentals=0
        ),
        compiler_params=pltpu.CompilerParams(vmem_limit_bytes=32 * 2**20),
    )(top, bottom, modulus, inside)


CHUNKS = (4608, 2304, 1152, 384, 128)


def densities(classes, level_density):
    levels = level_density.shape[0]
    level_index = lax.iota(jnp.int32, levels).reshape(levels, 1, 1)
    matches = classes[None] == level_index
    return jnp.sum(jnp.where(matches, level_density[:, None, None], 0.0), 0)


def split(x):
    upper = x.astype(jnp.bfloat16)
    lower = (x - upper.astype(jnp.float32)).astype(jnp.bfloat16)
    return jnp.concatenate([upper, lower], 0)


def gram_kernel(block_count, lanes_own, *refs):
    density_ref, stiff_ref, mass_ref = refs[4 * block_count :]

    def gathered(which, start):
        parts = refs[which * block_count : (which + 1) * block_count]
        return jnp.concatenate([ref[0, :, start : start + lanes_own] for ref in parts], 0)

    def product(a, b):
        return lax.dot_general(
            a, b, (((1,), (1,)), ((), ())), preferred_element_type=jnp.float32
        )

    def folded(wide):
        size = wide.shape[0] // 2
        return wide[:size, :size] + (wide[size:, :size] + wide[:size, size:])

    top = gathered(0, MARGIN)
    size = top.shape[0]
    right = [split(gathered(2, 0)), split(top * density_ref[...])]
    both = product(split(top), jnp.concatenate(right, 0))
    low = product(split(gathered(1, MARGIN)), split(gathered(3, 0)))
    stiff = folded(both[:, : 2 * size]) + folded(low)
    mass = folded(both[:, 2 * size :])

    @pl.when(pl.program_id(0) == 0)
    def first():
        stiff_ref[...] = stiff
        mass_ref[...] = mass

    @pl.when(pl.program_id(0) > 0)
    def later():
        stiff_ref[...] += stiff
        mass_ref[...] += mass


def grams(tops, bottoms, force_tops, force_bottoms, density):
    arrays = tops + bottoms + force_tops + force_bottoms
    size = sum(top.shape[1] for top in tops)
    shape = jax.ShapeDtypeStruct((size, size), jnp.float32)
    out_block = pl.BlockSpec((size, size), lambda c: (0, 0))
    return pl.pallas_call(
        functools.partial(gram_kernel, len(tops), density.shape[1]),
        grid=(tops[0].shape[0],),
        in_specs=[pl.BlockSpec((1,) + x.shape[1:], lambda c: (c, 0, 0)) for x in arrays]
        + [pl.BlockSpec(density.shape, lambda c: (0, 0))],
        out_specs=[out_block, out_block],
        out_shape=[shape, shape],
        cost_estimate=pl.CostEstimate(
            flops=5 * 10**9, bytes_accessed=10**7, transcendentals=0
        ),
        compiler_params=pltpu.CompilerParams(vmem_limit_bytes=48 * 2**20),
    )(*arrays, density)


def dot(a, b, contract):
    return lax.dot_general(
        a, b, ((contract[:1], contract[1:]), ((), ())), precision=highest,
        preferred_element_type=jnp.float32,
    )


def ritz_kernel(
    axes, mode_count, total_dofs, stiff_ref, mass_ref, ritz_ref, rotate_ref, mixed_ref,
    sums, landed, send_sem, recv_sem,
):
    size = stiff_ref.shape[0]
    groups = size // mode_count
    partners = []
    for name, count in axes:
        own = lax.axis_index(name)
        bit = 1
        while bit < count:
            set_here = lax.rem(lax.div(own, bit), 2)
            partners.append({name: own + bit - 2 * bit * set_here})
            bit *= 2
    barrier = pltpu.get_barrier_semaphore()
    for partner in partners:
        pl.semaphore_signal(
            barrier, inc=1, device_id=partner, device_id_type=pl.DeviceIdType.MESH
        )

    group = lax.axis_index("modes")
    row = lax.broadcasted_iota(jnp.int32, (size, size), 0)
    column = lax.broadcasted_iota(jnp.int32, (size, size), 1)
    place = jnp.zeros((size, size), jnp.float32)
    for s in range(groups):
        move = (lax.rem(group - s + groups, groups) - s) * mode_count
        here = (row >= s * mode_count) & (row < (s + 1) * mode_count) & (column - row == move)
        place = jnp.where(here, 1.0, place)

    sums[0, :, :size] = dot(dot(place, stiff_ref[...], (0, 0)), place, (1, 0))
    sums[0, :, size:] = dot(dot(place, mass_ref[...], (0, 0)), place, (1, 0))
    pl.semaphore_wait(barrier, len(partners))
    for step, partner in enumerate(partners):
        copy = pltpu.make_async_remote_copy(
            src_ref=sums.at[step],
            dst_ref=landed.at[step],
            send_sem=send_sem.at[step],
            recv_sem=recv_sem.at[step],
            device_id=partner,
            device_id_type=pl.DeviceIdType.MESH,
        )
        copy.start()
        copy.wait()
        sums[step + 1] = sums[step] + landed[step]
    total = sums[len(partners)] * (1.0 / total_dofs)
    gram_stiff = total[:, :size]

    lane = lax.broadcasted_iota(jnp.int32, (8, 2 * size), 1)
    sub = lax.broadcasted_iota(jnp.int32, (8, 2 * size), 0)
    blocks = []
    for block in range(size // 8):
        unit = jnp.where(lane == sub + 8 * block, 1.0, 0.0)
        blocks.append(jnp.where(lane < size, unit, total[8 * block : 8 * block + 8]))
    for k in range(size):
        at = k // 8
        pivot_row = blocks[at][k % 8 : k % 8 + 1]
        pivot_row = pivot_row / pivot_row[:, size + k : size + k + 1]
        for block in range(at, size // 8):
            factor = blocks[block][:, size + k : size + k + 1]
            if block == at:
                factor = jnp.where(sub[:, :1] > k % 8, factor, 0.0)
            blocks[block] = blocks[block] - factor * pivot_row
    rows = jnp.concatenate(blocks, 0)
    row = lax.broadcasted_iota(jnp.int32, (size, 2 * size), 0)
    column = lax.broadcasted_iota(jnp.int32, (size, 2 * size), 1)
    pivots = jnp.sum(jnp.where(column == row + size, rows, 0.0), 1, keepdims=True)
    inverse = rows[:, :size] * (1.0 / jnp.sqrt(pivots))
    ritz = dot(dot(inverse, gram_stiff, (1, 0)), inverse, (1, 1))
    ritz_ref[...] = ritz
    mixed = dot(ritz, inverse, (0, 0))
    rotate_ref[...] = dot(dot(place, inverse, (1, 0)), place, (1, 1))
    mixed_ref[...] = dot(dot(place, mixed, (1, 0)), place, (1, 1))


def ritz_solve(part_stiff, part_mass, mode_count, total_dofs):
    size = part_stiff.shape[0]
    axes = [(name, lax.axis_size(name)) for name in ("mesh", "modes")]
    steps = sum(count.bit_length() - 1 for name, count in axes)
    shape = jax.ShapeDtypeStruct((size, size), jnp.float32)
    whole = pl.BlockSpec(memory_space=pltpu.VMEM)
    return pl.pallas_call(
        functools.partial(ritz_kernel, axes, mode_count, total_dofs),
        in_specs=[whole, whole],
        out_specs=[whole] * 3,
        out_shape=[shape] * 3,
        scratch_shapes=[
            pltpu.VMEM((steps + 1, size, 2 * size), jnp.float32),
            pltpu.VMEM((steps, size, 2 * size), jnp.float32),
            pltpu.SemaphoreType.DMA((steps,)),
            pltpu.SemaphoreType.DMA((steps,)),
        ],
        cost_estimate=pl.CostEstimate(flops=10**7, bytes_accessed=10**5, transcendentals=0),
        compiler_params=pltpu.CompilerParams(collective_id=0, has_side_effects=True),
    )(part_stiff, part_mass)


def rotated(x, axis, by):
    size = lax.axis_size(axis)
    return lax.ppermute(x, axis, [(i, (i + by) % size) for i in range(size)])


def per_device(subspace, classes, level_density):
    mode_count, comps, plane_count, nodes = subspace.shape
    groups = lax.axis_size("modes")
    group = lax.axis_index("modes")
    total_dofs = comps * nodes * plane_count * lax.axis_size("mesh")
    lanes_own = nodes // groups
    wide = lanes_own + 2 * MARGIN

    density = densities(classes, level_density)
    modulus = floor_modulus + (1.0 - floor_modulus) * density * density * density
    own = group * lanes_own
    modulus = lax.dynamic_slice(jnp.pad(modulus, ((0, 0), (MARGIN, MARGIN))), (0, own), (1, wide))
    density = lax.dynamic_slice(density, (0, own), (1, lanes_own))
    inside = jnp.asarray(((np.arange(wide) - MARGIN) % NX >= 1)[None], jnp.float32)

    vectors = jnp.transpose(subspace[:, :, 0], (1, 0, 2))
    padded = jnp.pad(vectors, ((0, 0), (0, 0), (MARGIN, MARGIN)))
    pieces = 2 if mode_count % 16 == 0 else 1
    rows = mode_count // pieces
    tops = []
    for s in range(groups):
        target = lax.rem(group + s, groups)
        for piece in range(1 if s == 0 else pieces):
            size = mode_count if s == 0 else rows
            window = lax.dynamic_slice(
                padded, (0, piece * rows, target * lanes_own), (comps, size, wide)
            )
            tops.append(window if s == 0 else rotated(window, "modes", s))
    bottoms, force_tops, force_bottoms = [], [], []
    for index, top in enumerate(tops):
        if index >= 2:
            top, force_bottoms[0] = lax.optimization_barrier((top, force_bottoms[0]))
            tops[index] = top
        bottoms.append(shifted(top, "mesh", 1))
        force_top, force_bottom = layer_forces(top, bottoms[-1], modulus, inside)
        force_tops.append(force_top)
        force_bottoms.append(force_bottom)
    returned = [shifted(force, "mesh", -1) for force in force_bottoms]
    part_stiff, part_mass = grams(tops, bottoms, force_tops, force_bottoms, density)
    ritz_matrix, rotate, mixed_rotate = ritz_solve(part_stiff, part_mass, mode_count, total_dofs)
    middle = slice(MARGIN, MARGIN + lanes_own)
    mass = jnp.concatenate([t[:, :, middle] for t in tops], 1) * density
    image = jnp.concatenate([f + r for f, r in zip(force_tops, returned)], 1)
    parts = []
    for s in reversed(range(groups)):
        for piece in range(1 if s == 0 else pieces):
            size = mode_count if s == 0 else rows
            start = s * mode_count + piece * rows
            columns = slice(start, start + size)
            part = jnp.einsum("ckn,jk->jcn", image, rotate[columns], precision=high)
            part = part - jnp.einsum("ckn,jk->jcn", mass, mixed_rotate[columns], precision=high)
            parts.append((s, piece * rows, part if s == 0 else rotated(part, "modes", -s)))
    parts = parts[::-1]
    residual = jnp.zeros((mode_count, comps, nodes), jnp.float32)
    for s, start, part in parts:
        source = lax.rem(group + s, groups)
        residual = lax.dynamic_update_slice(residual, part, (start, 0, source * lanes_own))
    return (residual[:, :, None], ritz_matrix)


def solution(mesh):
    in_specs = (P("modes", None, "mesh", None), P("mesh", None), P())
    out_specs = (P("modes", None, "mesh", None), P())
    return jax.shard_map(
        per_device, mesh=mesh, in_specs=in_specs, out_specs=out_specs, check_vma=False
    )
```

```python
import functools

import jax
import jax.numpy as jnp
import numpy as np
from jax import lax
from jax.experimental import pallas as pl
from jax.experimental.pallas import tpu as pltpu
from jax.sharding import PartitionSpec as P

NX = 96
NY = 96


highest = lax.Precision.HIGHEST
high = lax.Precision.HIGH
MARGIN = 128
floor_modulus = 0.001


def shifted(x, axis, by):
    size = lax.axis_size(axis)
    pairs = [(i, i + by) for i in range(size) if 0 <= i + by < size]
    return lax.ppermute(x, axis, pairs)


def element_matrix():
    poisson_ratio = 0.3
    lame_first = poisson_ratio / ((1 + poisson_ratio) * (1 - 2 * poisson_ratio))
    shear_modulus = 1.0 / (2 * (1 + poisson_ratio))
    elastic = np.zeros((6, 6))
    elastic[:3, :3] = lame_first
    for normal_index in range(3):
        elastic[normal_index, normal_index] = lame_first + 2 * shear_modulus
        elastic[normal_index + 3, normal_index + 3] = shear_modulus
    corner_signs = [
        (1 - 2 * (corner & 1), 1 - 2 * (corner >> 1 & 1), 1 - 2 * (corner >> 2))
        for corner in range(8)
    ]
    gauss_point = 1.0 / np.sqrt(3.0)
    matrix = np.zeros((24, 24))
    for gauss_x in (-gauss_point, gauss_point):
        for gauss_y in (-gauss_point, gauss_point):
            for gauss_z in (-gauss_point, gauss_point):
                strain = np.zeros((6, 24))
                for corner in range(8):
                    sign_x, sign_y, sign_z = corner_signs[corner]
                    deriv_x = 2 * sign_x * (1 + sign_y * gauss_y) * (1 + sign_z * gauss_z) / 8
                    deriv_y = 2 * sign_y * (1 + sign_x * gauss_x) * (1 + sign_z * gauss_z) / 8
                    deriv_z = 2 * sign_z * (1 + sign_x * gauss_x) * (1 + sign_y * gauss_y) / 8
                    column = 3 * corner
                    strain[0, column] = deriv_x
                    strain[1, column + 1] = deriv_y
                    strain[2, column + 2] = deriv_z
                    strain[3, column] = deriv_y
                    strain[3, column + 1] = deriv_x
                    strain[4, column + 1] = deriv_z
                    strain[4, column + 2] = deriv_y
                    strain[5, column] = deriv_z
                    strain[5, column + 2] = deriv_x
                matrix = matrix + strain.T @ elastic @ strain / 8
    return matrix.reshape(8, 3, 8, 3)


def hadamard_matrix():
    signs = np.array([[1.0, 1.0], [1.0, -1.0]])
    transform = np.kron(np.kron(signs, signs), signs)
    matrix = np.einsum("ha,acbd,bg->hcgd", transform, element_matrix(), transform) / 64
    matrix[np.abs(matrix) < 1e-12] = 0.0
    return matrix


def layer_kernel(chunk, lanes_own, top_ref, bottom_ref, modulus_ref, inside_ref, out_top, out_bottom):
    matrix = hadamard_matrix()

    def step(index, carry):
        start = pl.multiple_of(index * chunk, 128)
        wide = chunk + 2 * MARGIN
        narrow = chunk + MARGIN
        inside = inside_ref[:, pl.ds(start, wide)]
        modulus = modulus_ref[:, pl.ds(start + MARGIN, narrow)]
        inside_narrow = inside[:, MARGIN:]
        hat = {}
        for c in range(3):
            top = top_ref[c, :, pl.ds(start, wide)]
            bottom = bottom_ref[c, :, pl.ds(start, wide)]
            for hz, plane in ((0, top + bottom), (1, top - bottom)):
                moved = pltpu.roll(plane, 1, 1) * inside
                for hx, line in ((0, plane + moved), (1, plane - moved)):
                    here = line[:, MARGIN:]
                    behind = pltpu.roll(line, NX, 1)[:, MARGIN:]
                    hat[hx + 4 * hz, c] = here + behind
                    hat[hx + 2 + 4 * hz, c] = here - behind

        def force(h, c):
            total = None
            for g in range(8):
                for d in range(3):
                    factor = float(matrix[h, c, g, d])
                    if factor != 0.0:
                        term = hat[g, d] * factor
                        total = term if total is None else total + term
            return None if total is None else total * modulus

        def both(first, second):
            if first is None:
                return second, -second
            return first + second, first - second

        for c in range(3):
            layers = []
            for hz in (0, 1):
                lines = []
                for hx in (0, 1):
                    near, far = both(force(hx + 4 * hz, c), force(hx + 2 + 4 * hz, c))
                    lines.append(near + pltpu.roll(far, narrow - NX, 1))
                near, far = both(lines[0], lines[1])
                layers.append((near + pltpu.roll(far * inside_narrow, narrow - 1, 1))[:, :chunk])
            out_top[c, :, pl.ds(start, chunk)] = layers[0] + layers[1]
            out_bottom[c, :, pl.ds(start, chunk)] = layers[0] - layers[1]
        return carry

    lax.fori_loop(0, lanes_own // chunk, step, 0)


def layer_forces(top, bottom, modulus, inside):
    comps, mode_count, wide = top.shape
    lanes_own = wide - 2 * MARGIN
    chunk = next(size for size in CHUNKS if lanes_own % size == 0)
    rows = 8
    in_block = pl.BlockSpec((comps, rows, wide), lambda m: (0, m, 0))
    row_block = pl.BlockSpec((1, wide), lambda m: (0, 0))
    out_block = pl.BlockSpec((comps, rows, lanes_own), lambda m: (0, m, 0))
    shape = jax.ShapeDtypeStruct((comps, mode_count, lanes_own), jnp.float32)
    return pl.pallas_call(
        functools.partial(layer_kernel, chunk, lanes_own),
        grid=(mode_count // rows,),
        in_specs=[in_block, in_block, row_block, row_block],
        out_specs=[out_block, out_block],
        out_shape=[shape, shape],
        cost_estimate=pl.CostEstimate(
            flops=36000 * top.size, bytes_accessed=16 * top.size, transcendentals=0
        ),
        compiler_params=pltpu.CompilerParams(vmem_limit_bytes=32 * 2**20),
    )(top, bottom, modulus, inside)


CHUNKS = (4608, 2304, 1152, 384, 128)


def densities(classes, level_density):
    levels = level_density.shape[0]
    level_index = lax.iota(jnp.int32, levels).reshape(levels, 1, 1)
    matches = classes[None] == level_index
    return jnp.sum(jnp.where(matches, level_density[:, None, None], 0.0), 0)


def split(x):
    upper = x.astype(jnp.bfloat16)
    lower = (x - upper.astype(jnp.float32)).astype(jnp.bfloat16)
    return jnp.concatenate([upper, lower], 0)


def gram_kernel(block_count, lanes_own, *refs):
    density_ref, stiff_ref, mass_ref = refs[4 * block_count :]

    def gathered(which, start):
        parts = refs[which * block_count : (which + 1) * block_count]
        return jnp.concatenate([ref[0, :, start : start + lanes_own] for ref in parts], 0)

    def product(a, b):
        return lax.dot_general(
            a, b, (((1,), (1,)), ((), ())), preferred_element_type=jnp.float32
        )

    def folded(wide):
        size = wide.shape[0] // 2
        return wide[:size, :size] + (wide[size:, :size] + wide[:size, size:])

    top = gathered(0, MARGIN)
    size = top.shape[0]
    right = [split(gathered(2, 0)), split(top * density_ref[...])]
    both = product(split(top), jnp.concatenate(right, 0))
    low = product(split(gathered(1, MARGIN)), split(gathered(3, 0)))
    stiff = folded(both[:, : 2 * size]) + folded(low)
    mass = folded(both[:, 2 * size :])

    @pl.when(pl.program_id(0) == 0)
    def first():
        stiff_ref[...] = stiff
        mass_ref[...] = mass

    @pl.when(pl.program_id(0) > 0)
    def later():
        stiff_ref[...] += stiff
        mass_ref[...] += mass


def grams(tops, bottoms, force_tops, force_bottoms, density):
    arrays = tops + bottoms + force_tops + force_bottoms
    size = sum(top.shape[1] for top in tops)
    shape = jax.ShapeDtypeStruct((size, size), jnp.float32)
    out_block = pl.BlockSpec((size, size), lambda c: (0, 0))
    return pl.pallas_call(
        functools.partial(gram_kernel, len(tops), density.shape[1]),
        grid=(tops[0].shape[0],),
        in_specs=[pl.BlockSpec((1,) + x.shape[1:], lambda c: (c, 0, 0)) for x in arrays]
        + [pl.BlockSpec(density.shape, lambda c: (0, 0))],
        out_specs=[out_block, out_block],
        out_shape=[shape, shape],
        cost_estimate=pl.CostEstimate(
            flops=5 * 10**9, bytes_accessed=10**7, transcendentals=0
        ),
        compiler_params=pltpu.CompilerParams(vmem_limit_bytes=48 * 2**20),
    )(*arrays, density)


def dot(a, b, contract):
    return lax.dot_general(
        a, b, ((contract[:1], contract[1:]), ((), ())), precision=highest,
        preferred_element_type=jnp.float32,
    )


def ritz_kernel(
    axes, mode_count, total_dofs, stiff_ref, mass_ref, ritz_ref, rotate_ref, mixed_ref,
    sums, landed, send_sem, recv_sem,
):
    size = stiff_ref.shape[0]
    groups = size // mode_count
    partners = []
    for name, count in axes:
        own = lax.axis_index(name)
        bit = 1
        while bit < count:
            set_here = lax.rem(lax.div(own, bit), 2)
            partners.append({name: own + bit - 2 * bit * set_here})
            bit *= 2
    barrier = pltpu.get_barrier_semaphore()
    for partner in partners:
        pl.semaphore_signal(
            barrier, inc=1, device_id=partner, device_id_type=pl.DeviceIdType.MESH
        )

    group = lax.axis_index("modes")
    row = lax.broadcasted_iota(jnp.int32, (size, size), 0)
    column = lax.broadcasted_iota(jnp.int32, (size, size), 1)
    place = jnp.zeros((size, size), jnp.float32)
    for s in range(groups):
        move = (lax.rem(group - s + groups, groups) - s) * mode_count
        here = (row >= s * mode_count) & (row < (s + 1) * mode_count) & (column - row == move)
        place = jnp.where(here, 1.0, place)

    sums[0, :, :size] = dot(dot(place, stiff_ref[...], (0, 0)), place, (1, 0))
    sums[0, :, size:] = dot(dot(place, mass_ref[...], (0, 0)), place, (1, 0))
    pl.semaphore_wait(barrier, len(partners))
    for step, partner in enumerate(partners):
        copy = pltpu.make_async_remote_copy(
            src_ref=sums.at[step],
            dst_ref=landed.at[step],
            send_sem=send_sem.at[step],
            recv_sem=recv_sem.at[step],
            device_id=partner,
            device_id_type=pl.DeviceIdType.MESH,
        )
        copy.start()
        copy.wait()
        sums[step + 1] = sums[step] + landed[step]
    total = sums[len(partners)] * (1.0 / total_dofs)
    gram_stiff = total[:, :size]

    lane = lax.broadcasted_iota(jnp.int32, (8, 2 * size), 1)
    sub = lax.broadcasted_iota(jnp.int32, (8, 2 * size), 0)
    blocks = []
    for block in range(size // 8):
        unit = jnp.where(lane == sub + 8 * block, 1.0, 0.0)
        blocks.append(jnp.where(lane < size, unit, total[8 * block : 8 * block + 8]))
    for k in range(size):
        at = k // 8
        pivot_row = blocks[at][k % 8 : k % 8 + 1]
        pivot_row = pivot_row / pivot_row[:, size + k : size + k + 1]
        for block in range(at, size // 8):
            factor = blocks[block][:, size + k : size + k + 1]
            if block == at:
                factor = jnp.where(sub[:, :1] > k % 8, factor, 0.0)
            blocks[block] = blocks[block] - factor * pivot_row
    rows = jnp.concatenate(blocks, 0)
    row = lax.broadcasted_iota(jnp.int32, (size, 2 * size), 0)
    column = lax.broadcasted_iota(jnp.int32, (size, 2 * size), 1)
    pivots = jnp.sum(jnp.where(column == row + size, rows, 0.0), 1, keepdims=True)
    inverse = rows[:, :size] * (1.0 / jnp.sqrt(pivots))
    ritz = dot(dot(inverse, gram_stiff, (1, 0)), inverse, (1, 1))
    ritz_ref[...] = ritz
    mixed = dot(ritz, inverse, (0, 0))
    rotate_ref[...] = dot(dot(place, inverse, (1, 0)), place, (1, 1))
    mixed_ref[...] = dot(dot(place, mixed, (1, 0)), place, (1, 1))


def ritz_solve(part_stiff, part_mass, mode_count, total_dofs):
    size = part_stiff.shape[0]
    axes = [(name, lax.axis_size(name)) for name in ("mesh", "modes")]
    steps = sum(count.bit_length() - 1 for name, count in axes)
    shape = jax.ShapeDtypeStruct((size, size), jnp.float32)
    whole = pl.BlockSpec(memory_space=pltpu.VMEM)
    return pl.pallas_call(
        functools.partial(ritz_kernel, axes, mode_count, total_dofs),
        in_specs=[whole, whole],
        out_specs=[whole] * 3,
        out_shape=[shape] * 3,
        scratch_shapes=[
            pltpu.VMEM((steps + 1, size, 2 * size), jnp.float32),
            pltpu.VMEM((steps, size, 2 * size), jnp.float32),
            pltpu.SemaphoreType.DMA((steps,)),
            pltpu.SemaphoreType.DMA((steps,)),
        ],
        cost_estimate=pl.CostEstimate(flops=10**7, bytes_accessed=10**5, transcendentals=0),
        compiler_params=pltpu.CompilerParams(collective_id=0, has_side_effects=True),
    )(part_stiff, part_mass)


def rotated(x, axis, by):
    size = lax.axis_size(axis)
    return lax.ppermute(x, axis, [(i, (i + by) % size) for i in range(size)])


def per_device(subspace, classes, level_density):
    mode_count, comps, plane_count, nodes = subspace.shape
    groups = lax.axis_size("modes")
    group = lax.axis_index("modes")
    total_dofs = comps * nodes * plane_count * lax.axis_size("mesh")
    lanes_own = nodes // groups
    wide = lanes_own + 2 * MARGIN

    density = densities(classes, level_density)
    modulus = floor_modulus + (1.0 - floor_modulus) * density * density * density
    own = group * lanes_own
    modulus = lax.dynamic_slice(jnp.pad(modulus, ((0, 0), (MARGIN, MARGIN))), (0, own), (1, wide))
    density = lax.dynamic_slice(density, (0, own), (1, lanes_own))
    inside = jnp.asarray(((np.arange(wide) - MARGIN) % NX >= 1)[None], jnp.float32)

    vectors = jnp.transpose(subspace[:, :, 0], (1, 0, 2))
    padded = jnp.pad(vectors, ((0, 0), (0, 0), (MARGIN, MARGIN)))
    pieces = 2 if mode_count % 16 == 0 else 1
    rows = mode_count // pieces
    tops, bottoms, force_tops, force_bottoms = [], [], [], []
    for s in range(groups):
        target = lax.rem(group + s, groups)
        for piece in range(1 if s == 0 else pieces):
            size = mode_count if s == 0 else rows
            window = lax.dynamic_slice(
                padded, (0, piece * rows, target * lanes_own), (comps, size, wide)
            )
            if s > 0:
                if len(tops) >= 2:
                    window, tops[-1] = lax.optimization_barrier((window, tops[-1]))
                window = rotated(window, "modes", s)
            tops.append(window)
    for index in range(len(tops)):
        if index >= 2:
            tops[index], force_bottoms[-1] = lax.optimization_barrier(
                (tops[index], force_bottoms[-1])
            )
        bottoms.append(shifted(tops[index], "mesh", 1))
        force_top, force_bottom = layer_forces(tops[index], bottoms[-1], modulus, inside)
        force_tops.append(force_top)
        force_bottoms.append(force_bottom)
    returned = [shifted(force, "mesh", -1) for force in force_bottoms]
    part_stiff, part_mass = grams(tops, bottoms, force_tops, force_bottoms, density)
    ritz_matrix, rotate, mixed_rotate = ritz_solve(part_stiff, part_mass, mode_count, total_dofs)
    middle = slice(MARGIN, MARGIN + lanes_own)
    mass = jnp.concatenate([t[:, :, middle] for t in tops], 1) * density
    image = jnp.concatenate(force_tops, 1) + jnp.concatenate(returned, 1)
    parts = []
    for s in reversed(range(groups)):
        columns = slice(s * mode_count, (s + 1) * mode_count)
        part = jnp.einsum("ckn,jk->jcn", image, rotate[columns], precision=high)
        part = part - jnp.einsum("ckn,jk->jcn", mass, mixed_rotate[columns], precision=high)
        parts.append(part if s == 0 else rotated(part, "modes", -s))
    parts = parts[::-1]
    residual = jnp.zeros((mode_count, comps, nodes), jnp.float32)
    for s, part in enumerate(parts):
        source = lax.rem(group + s, groups)
        residual = lax.dynamic_update_slice(residual, part, (0, 0, source * lanes_own))
    return (residual[:, :, None], ritz_matrix)


def solution(mesh):
    in_specs = (P("modes", None, "mesh", None), P("mesh", None), P())
    out_specs = (P("modes", None, "mesh", None), P())
    return jax.shard_map(
        per_device, mesh=mesh, in_specs=in_specs, out_specs=out_specs, check_vma=False
    )
```

```python
import functools

import jax
import jax.numpy as jnp
import numpy as np
from jax import lax
from jax.experimental import pallas as pl
from jax.experimental.pallas import tpu as pltpu
from jax.sharding import PartitionSpec as P

NX = 96
NY = 96


highest = lax.Precision.HIGHEST
high = lax.Precision.HIGH
MARGIN = 128
floor_modulus = 0.001


def shifted(x, axis, by):
    size = lax.axis_size(axis)
    pairs = [(i, i + by) for i in range(size) if 0 <= i + by < size]
    return lax.ppermute(x, axis, pairs)


def element_matrix():
    poisson_ratio = 0.3
    lame_first = poisson_ratio / ((1 + poisson_ratio) * (1 - 2 * poisson_ratio))
    shear_modulus = 1.0 / (2 * (1 + poisson_ratio))
    elastic = np.zeros((6, 6))
    elastic[:3, :3] = lame_first
    for normal_index in range(3):
        elastic[normal_index, normal_index] = lame_first + 2 * shear_modulus
        elastic[normal_index + 3, normal_index + 3] = shear_modulus
    corner_signs = [
        (1 - 2 * (corner & 1), 1 - 2 * (corner >> 1 & 1), 1 - 2 * (corner >> 2))
        for corner in range(8)
    ]
    gauss_point = 1.0 / np.sqrt(3.0)
    matrix = np.zeros((24, 24))
    for gauss_x in (-gauss_point, gauss_point):
        for gauss_y in (-gauss_point, gauss_point):
            for gauss_z in (-gauss_point, gauss_point):
                strain = np.zeros((6, 24))
                for corner in range(8):
                    sign_x, sign_y, sign_z = corner_signs[corner]
                    deriv_x = 2 * sign_x * (1 + sign_y * gauss_y) * (1 + sign_z * gauss_z) / 8
                    deriv_y = 2 * sign_y * (1 + sign_x * gauss_x) * (1 + sign_z * gauss_z) / 8
                    deriv_z = 2 * sign_z * (1 + sign_x * gauss_x) * (1 + sign_y * gauss_y) / 8
                    column = 3 * corner
                    strain[0, column] = deriv_x
                    strain[1, column + 1] = deriv_y
                    strain[2, column + 2] = deriv_z
                    strain[3, column] = deriv_y
                    strain[3, column + 1] = deriv_x
                    strain[4, column + 1] = deriv_z
                    strain[4, column + 2] = deriv_y
                    strain[5, column] = deriv_z
                    strain[5, column + 2] = deriv_x
                matrix = matrix + strain.T @ elastic @ strain / 8
    return matrix.reshape(8, 3, 8, 3)


def hadamard_matrix():
    signs = np.array([[1.0, 1.0], [1.0, -1.0]])
    transform = np.kron(np.kron(signs, signs), signs)
    matrix = np.einsum("ha,acbd,bg->hcgd", transform, element_matrix(), transform) / 64
    matrix[np.abs(matrix) < 1e-12] = 0.0
    return matrix


def layer_kernel(chunk, lanes_own, top_ref, bottom_ref, modulus_ref, inside_ref, out_top, out_bottom):
    matrix = hadamard_matrix()

    def step(index, carry):
        start = pl.multiple_of(index * chunk, 128)
        wide = chunk + 2 * MARGIN
        narrow = chunk + MARGIN
        inside = inside_ref[:, pl.ds(start, wide)]
        modulus = modulus_ref[:, pl.ds(start + MARGIN, narrow)]
        inside_narrow = inside[:, MARGIN:]
        hat = {}
        for c in range(3):
            top = top_ref[c, :, pl.ds(start, wide)]
            bottom = bottom_ref[c, :, pl.ds(start, wide)]
            for hz, plane in ((0, top + bottom), (1, top - bottom)):
                moved = pltpu.roll(plane, 1, 1) * inside
                for hx, line in ((0, plane + moved), (1, plane - moved)):
                    here = line[:, MARGIN:]
                    behind = pltpu.roll(line, NX, 1)[:, MARGIN:]
                    hat[hx + 4 * hz, c] = here + behind
                    hat[hx + 2 + 4 * hz, c] = here - behind

        def force(h, c):
            total = None
            for g in range(8):
                for d in range(3):
                    factor = float(matrix[h, c, g, d])
                    if factor != 0.0:
                        term = hat[g, d] * factor
                        total = term if total is None else total + term
            return None if total is None else total * modulus

        def both(first, second):
            if first is None:
                return second, -second
            return first + second, first - second

        for c in range(3):
            layers = []
            for hz in (0, 1):
                lines = []
                for hx in (0, 1):
                    near, far = both(force(hx + 4 * hz, c), force(hx + 2 + 4 * hz, c))
                    lines.append(near + pltpu.roll(far, narrow - NX, 1))
                near, far = both(lines[0], lines[1])
                layers.append((near + pltpu.roll(far * inside_narrow, narrow - 1, 1))[:, :chunk])
            out_top[c, :, pl.ds(start, chunk)] = layers[0] + layers[1]
            out_bottom[c, :, pl.ds(start, chunk)] = layers[0] - layers[1]
        return carry

    lax.fori_loop(0, lanes_own // chunk, step, 0)


def layer_forces(top, bottom, modulus, inside):
    comps, mode_count, wide = top.shape
    lanes_own = wide - 2 * MARGIN
    chunk = next(size for size in CHUNKS if lanes_own % size == 0)
    rows = 8
    in_block = pl.BlockSpec((comps, rows, wide), lambda m: (0, m, 0))
    row_block = pl.BlockSpec((1, wide), lambda m: (0, 0))
    out_block = pl.BlockSpec((comps, rows, lanes_own), lambda m: (0, m, 0))
    shape = jax.ShapeDtypeStruct((comps, mode_count, lanes_own), jnp.float32)
    return pl.pallas_call(
        functools.partial(layer_kernel, chunk, lanes_own),
        grid=(mode_count // rows,),
        in_specs=[in_block, in_block, row_block, row_block],
        out_specs=[out_block, out_block],
        out_shape=[shape, shape],
        cost_estimate=pl.CostEstimate(
            flops=36000 * top.size, bytes_accessed=16 * top.size, transcendentals=0
        ),
        compiler_params=pltpu.CompilerParams(vmem_limit_bytes=32 * 2**20),
    )(top, bottom, modulus, inside)


CHUNKS = (4608, 2304, 1152, 384, 128)


def densities(classes, level_density):
    levels = level_density.shape[0]
    level_index = lax.iota(jnp.int32, levels).reshape(levels, 1, 1)
    matches = classes[None] == level_index
    return jnp.sum(jnp.where(matches, level_density[:, None, None], 0.0), 0)


def split(x):
    upper = x.astype(jnp.bfloat16)
    lower = (x - upper.astype(jnp.float32)).astype(jnp.bfloat16)
    return jnp.concatenate([upper, lower], 0)


def gram_kernel(block_count, lanes_own, *refs):
    density_ref, stiff_ref, mass_ref = refs[4 * block_count :]

    def gathered(which, start):
        parts = refs[which * block_count : (which + 1) * block_count]
        return jnp.concatenate([ref[0, :, start : start + lanes_own] for ref in parts], 0)

    def product(a, b):
        return lax.dot_general(
            a, b, (((1,), (1,)), ((), ())), preferred_element_type=jnp.float32
        )

    def folded(wide):
        size = wide.shape[0] // 2
        return wide[:size, :size] + (wide[size:, :size] + wide[:size, size:])

    top = gathered(0, MARGIN)
    size = top.shape[0]
    right = [split(gathered(2, 0)), split(top * density_ref[...])]
    both = product(split(top), jnp.concatenate(right, 0))
    low = product(split(gathered(1, MARGIN)), split(gathered(3, 0)))
    stiff = folded(both[:, : 2 * size]) + folded(low)
    mass = folded(both[:, 2 * size :])

    @pl.when(pl.program_id(0) == 0)
    def first():
        stiff_ref[...] = stiff
        mass_ref[...] = mass

    @pl.when(pl.program_id(0) > 0)
    def later():
        stiff_ref[...] += stiff
        mass_ref[...] += mass


def grams(tops, bottoms, force_tops, force_bottoms, density):
    arrays = tops + bottoms + force_tops + force_bottoms
    size = sum(top.shape[1] for top in tops)
    shape = jax.ShapeDtypeStruct((size, size), jnp.float32)
    out_block = pl.BlockSpec((size, size), lambda c: (0, 0))
    return pl.pallas_call(
        functools.partial(gram_kernel, len(tops), density.shape[1]),
        grid=(tops[0].shape[0],),
        in_specs=[pl.BlockSpec((1,) + x.shape[1:], lambda c: (c, 0, 0)) for x in arrays]
        + [pl.BlockSpec(density.shape, lambda c: (0, 0))],
        out_specs=[out_block, out_block],
        out_shape=[shape, shape],
        cost_estimate=pl.CostEstimate(
            flops=5 * 10**9, bytes_accessed=10**7, transcendentals=0
        ),
        compiler_params=pltpu.CompilerParams(vmem_limit_bytes=48 * 2**20),
    )(*arrays, density)


def dot(a, b, contract):
    return lax.dot_general(
        a, b, ((contract[:1], contract[1:]), ((), ())), precision=highest,
        preferred_element_type=jnp.float32,
    )


def ritz_kernel(
    axes, mode_count, total_dofs, stiff_ref, mass_ref, ritz_ref, rotate_ref, mixed_ref,
    sums, landed, send_sem, recv_sem,
):
    size = stiff_ref.shape[0]
    groups = size // mode_count
    partners = []
    for name, count in axes:
        own = lax.axis_index(name)
        bit = 1
        while bit < count:
            set_here = lax.rem(lax.div(own, bit), 2)
            partners.append({name: own + bit - 2 * bit * set_here})
            bit *= 2
    barrier = pltpu.get_barrier_semaphore()
    for partner in partners:
        pl.semaphore_signal(
            barrier, inc=1, device_id=partner, device_id_type=pl.DeviceIdType.MESH
        )

    group = lax.axis_index("modes")
    row = lax.broadcasted_iota(jnp.int32, (size, size), 0)
    column = lax.broadcasted_iota(jnp.int32, (size, size), 1)
    place = jnp.zeros((size, size), jnp.float32)
    for s in range(groups):
        move = (lax.rem(group - s + groups, groups) - s) * mode_count
        here = (row >= s * mode_count) & (row < (s + 1) * mode_count) & (column - row == move)
        place = jnp.where(here, 1.0, place)

    sums[0, :, :size] = dot(dot(place, stiff_ref[...], (0, 0)), place, (1, 0))
    sums[0, :, size:] = dot(dot(place, mass_ref[...], (0, 0)), place, (1, 0))
    pl.semaphore_wait(barrier, len(partners))
    for step, partner in enumerate(partners):
        copy = pltpu.make_async_remote_copy(
            src_ref=sums.at[step],
            dst_ref=landed.at[step],
            send_sem=send_sem.at[step],
            recv_sem=recv_sem.at[step],
            device_id=partner,
            device_id_type=pl.DeviceIdType.MESH,
        )
        copy.start()
        copy.wait()
        sums[step + 1] = sums[step] + landed[step]
    total = sums[len(partners)] * (1.0 / total_dofs)
    gram_stiff = total[:, :size]

    lane = lax.broadcasted_iota(jnp.int32, (8, 2 * size), 1)
    sub = lax.broadcasted_iota(jnp.int32, (8, 2 * size), 0)
    blocks = []
    for block in range(size // 8):
        unit = jnp.where(lane == sub + 8 * block, 1.0, 0.0)
        blocks.append(jnp.where(lane < size, unit, total[8 * block : 8 * block + 8]))
    for k in range(size):
        at = k // 8
        pivot_row = blocks[at][k % 8 : k % 8 + 1]
        pivot_row = pivot_row / pivot_row[:, size + k : size + k + 1]
        for block in range(at, size // 8):
            factor = blocks[block][:, size + k : size + k + 1]
            if block == at:
                factor = jnp.where(sub[:, :1] > k % 8, factor, 0.0)
            blocks[block] = blocks[block] - factor * pivot_row
    rows = jnp.concatenate(blocks, 0)
    row = lax.broadcasted_iota(jnp.int32, (size, 2 * size), 0)
    column = lax.broadcasted_iota(jnp.int32, (size, 2 * size), 1)
    pivots = jnp.sum(jnp.where(column == row + size, rows, 0.0), 1, keepdims=True)
    inverse = rows[:, :size] * (1.0 / jnp.sqrt(pivots))
    ritz = dot(dot(inverse, gram_stiff, (1, 0)), inverse, (1, 1))
    ritz_ref[...] = ritz
    mixed = dot(ritz, inverse, (0, 0))
    rotate_ref[...] = dot(dot(place, inverse, (1, 0)), place, (1, 1))
    mixed_ref[...] = dot(dot(place, mixed, (1, 0)), place, (1, 1))


def ritz_solve(part_stiff, part_mass, mode_count, total_dofs):
    size = part_stiff.shape[0]
    axes = [(name, lax.axis_size(name)) for name in ("mesh", "modes")]
    steps = sum(count.bit_length() - 1 for name, count in axes)
    shape = jax.ShapeDtypeStruct((size, size), jnp.float32)
    whole = pl.BlockSpec(memory_space=pltpu.VMEM)
    return pl.pallas_call(
        functools.partial(ritz_kernel, axes, mode_count, total_dofs),
        in_specs=[whole, whole],
        out_specs=[whole] * 3,
        out_shape=[shape] * 3,
        scratch_shapes=[
            pltpu.VMEM((steps + 1, size, 2 * size), jnp.float32),
            pltpu.VMEM((steps, size, 2 * size), jnp.float32),
            pltpu.SemaphoreType.DMA((steps,)),
            pltpu.SemaphoreType.DMA((steps,)),
        ],
        cost_estimate=pl.CostEstimate(flops=10**7, bytes_accessed=10**5, transcendentals=0),
        compiler_params=pltpu.CompilerParams(collective_id=0, has_side_effects=True),
    )(part_stiff, part_mass)


def rotated(x, axis, by):
    size = lax.axis_size(axis)
    return lax.ppermute(x, axis, [(i, (i + by) % size) for i in range(size)])


def per_device(subspace, classes, level_density):
    mode_count, comps, plane_count, nodes = subspace.shape
    groups = lax.axis_size("modes")
    group = lax.axis_index("modes")
    total_dofs = comps * nodes * plane_count * lax.axis_size("mesh")
    lanes_own = nodes // groups
    wide = lanes_own + 2 * MARGIN

    density = densities(classes, level_density)
    modulus = floor_modulus + (1.0 - floor_modulus) * density * density * density
    own = group * lanes_own
    modulus = lax.dynamic_slice(jnp.pad(modulus, ((0, 0), (MARGIN, MARGIN))), (0, own), (1, wide))
    density = lax.dynamic_slice(density, (0, own), (1, lanes_own))
    inside = jnp.asarray(((np.arange(wide) - MARGIN) % NX >= 1)[None], jnp.float32)

    vectors = jnp.transpose(subspace[:, :, 0], (1, 0, 2))
    padded = jnp.pad(vectors, ((0, 0), (0, 0), (MARGIN, MARGIN)))
    pieces = 2 if mode_count % 16 == 0 else 1
    rows = mode_count // pieces
    middle = slice(MARGIN, MARGIN + lanes_own)
    tops, bottoms, force_tops, force_bottoms = [], [], [], []
    for s in range(groups):
        target = lax.rem(group + s, groups)
        for piece in range(1 if s == 0 else pieces):
            size = mode_count if s == 0 else rows
            window = lax.dynamic_slice(
                padded, (0, piece * rows, target * lanes_own), (comps, size, wide)
            )
            if s > 0:
                if len(tops) >= 2:
                    window, tops[-1] = lax.optimization_barrier((window, tops[-1]))
                window = rotated(window, "modes", s)
            tops.append(window)
    for index in range(len(tops)):
        if index >= 2:
            tops[index], force_bottoms[-1], force_bottoms[0] = lax.optimization_barrier(
                (tops[index], force_bottoms[-1], force_bottoms[0])
            )
        bottoms.append(shifted(tops[index], "mesh", 1))
        if index == len(tops) - 1:
            mass = jnp.concatenate([t[:, :, middle] for t in tops], 1) * density
            mass, bottoms[-1] = lax.optimization_barrier((mass, bottoms[-1]))
        force_top, force_bottom = layer_forces(tops[index], bottoms[-1], modulus, inside)
        force_tops.append(force_top)
        force_bottoms.append(force_bottom)
    returned = [shifted(force, "mesh", -1) for force in force_bottoms]
    part_stiff, part_mass = grams(tops, bottoms, force_tops, force_bottoms, density)
    ritz_matrix, rotate, mixed_rotate = ritz_solve(part_stiff, part_mass, mode_count, total_dofs)
    image = jnp.concatenate(force_tops, 1) + jnp.concatenate(returned, 1)
    parts = []
    for s in reversed(range(groups)):
        columns = slice(s * mode_count, (s + 1) * mode_count)
        part = jnp.einsum("ckn,jk->jcn", image, rotate[columns], precision=high)
        part = part - jnp.einsum("ckn,jk->jcn", mass, mixed_rotate[columns], precision=high)
        parts.append(part if s == 0 else rotated(part, "modes", -s))
    parts = parts[::-1]
    residual = jnp.zeros((mode_count, comps, nodes), jnp.float32)
    for s, part in enumerate(parts):
        source = lax.rem(group + s, groups)
        residual = lax.dynamic_update_slice(residual, part, (0, 0, source * lanes_own))
    return (residual[:, :, None], ritz_matrix)


def solution(mesh):
    in_specs = (P("modes", None, "mesh", None), P("mesh", None), P())
    out_specs = (P("modes", None, "mesh", None), P())
    return jax.shard_map(
        per_device, mesh=mesh, in_specs=in_specs, out_specs=out_specs, check_vma=False
    )
```
